32 devices in a mesh: case: 2 (over x), box: 16 (over z, y, core).
Axes of the slice: x: 2, y: 2, z: 4, core: 2. Of those that a mesh axis runs over, the one named last changes fastest.
Arguments:
- sym_press: float32 [4, 64, 8192], P('case', None, 'box'), parts along dimension 0, may hold values from -0.15625 to 0.15625
- anti_press: float32 [4, 64, 8192], P('case', None, 'box'), parts along dimension 0, may hold values from -0.15625 to 0.15625
- box_geom: float32 [3, 8192], P(None, 'box'), may hold values from 0.25 to 2
- box_station: int32 [8192], P('box'), may hold values from 0 to 31, as said below
- station_geom: float32 [2, 32], P(None, 'box'), may hold values from 0.25 to 2
- gust_index: int32 [64], replicated, may hold values from 0 to 255
Outputs:
- load_hist: bfloat16 [64, 3, 2, 64, 512], P(('case', 'box')), parts along dimension 0
The draws below stay inside these ranges and needn't reach their ends.
There are 2 independent parts, one for each index of `case`. The reference program is written for one: setup_inputs(seed, part) draws one part's arguments, and reference() takes and returns one part's arrays. A program takes and returns all parts, laid end to end along the dimension named above; an argument that names none is the same for every part. Nothing has to cross between parts.
Inputs may be any that keep to these rules, and one draw needn't show every extreme that they name: `box_station`: station ids never fall along the boxes; the first box of station s lies in box block s // 2 (boxes d * 512 to (d + 1) * 512 - 1 hold the first boxes of stations d * 2 to (d + 1) * 2 - 1, and their other boxes belong to station d * 2 - 1; box 0 always opens station 0).
All inputs are finite; a program needn't handle non-finite values.
Results may differ from the reference program's by a relative error of at most 0.0086.
Values sent between devices are 32-bit elements; how exact they have to be, the bound alone decides.
No kernel may reach another device: no remote copies, remote signals or barrier semaphores. Data moves between devices by JAX's collectives and lax.ppermute only.
A program may use at most 64 MiB of HBM per device.

```python
import math
import jax
import jax.numpy as jnp
from jax import lax

F = 64
NFFT = 512
NG = 256
G = 64
BOX_DEV = 512
S_DEV = 2
BOXES = 8192
S = 32


def draw_box_station(key, part):
    key = jax.random.fold_in(key, 11)
    blocks = BOXES // BOX_DEV
    jitter = jax.random.randint(key, (blocks, BOX_DEV), 0, 65536)
    position = jnp.arange(BOX_DEV, dtype=jnp.int32)
    scores = jitter * BOX_DEV + position[None, :]
    opening = (jnp.arange(blocks, dtype=jnp.int32)[:, None] == 0) & (position[None, :] == 0)
    scores = jnp.where(opening, 65536 * BOX_DEV, scores)
    starts = lax.top_k(scores, S_DEV)[1].astype(jnp.int32)
    counted = jnp.sum((position[None, None, :] >= starts[:, :, None]).astype(jnp.int32), 1)
    station_ids = jnp.arange(blocks, dtype=jnp.int32)[:, None] * S_DEV - 1 + counted
    return station_ids.reshape(BOXES).astype(jnp.int32)


def place_ends(array, rng, smallest, high):
    extent = array.shape
    spot = [jax.random.randint(jax.random.fold_in(rng, axis), (), 0, extent[axis]) for axis in range(len(extent))]
    array = array.at[tuple(spot)].set(smallest)
    longest = extent.index(max(extent))
    spot[longest] = (spot[longest] + 1) % extent[longest]
    return array.at[tuple(spot)].set(high)


def block_levels(rng, extent, shards, smallest, top_value):
    loudness, own = 1.0, jax.random.fold_in(rng, 6)
    for dim, shards_of in shards:
        heights = jnp.exp(jax.random.uniform(jax.random.fold_in(own, dim), (shards_of,), jnp.float32, smallest / len(shards), top_value / len(shards)))
        loudness = loudness * jnp.repeat(heights, extent[dim] // shards_of).reshape([-1 if axis == dim else 1 for axis in range(len(extent))])
    return loudness


def bell_draw(own_key, dims, deviation, most, pieces=(), kind=jnp.bfloat16):
    loudness = block_levels(own_key, dims, pieces, -0.22, 0.18) if pieces else 1.0
    drawn = jax.random.normal(own_key, dims, jnp.float32) * deviation * loudness
    return jnp.minimum(jnp.maximum(drawn, -most), most).astype(kind)


def setup_inputs(seed: int = 0, part: int = 0) -> dict:
    key_of = jax.random.split(jax.random.key(seed), 7)
    own_keys = jax.random.split(jax.random.fold_in(key_of[6], part), 7)
    sym_press = bell_draw(own_keys[0], (2, F, BOXES), (BOXES ** -0.5), 0.15625, ((2, 16),), jnp.float32)
    anti_press = bell_draw(own_keys[1], (2, F, BOXES), (BOXES ** -0.5), 0.15625, ((2, 16),), jnp.float32)
    box_geom = jnp.clip(0.25 + 1.75 * jax.random.uniform(key_of[2], (3, BOXES), jnp.float32) ** block_levels(key_of[2], (3, BOXES), ((1, 16),), -0.2, 0.2), 0.25, 2.0)
    box_station = draw_box_station(jax.random.fold_in(key_of[6], 71), part)
    station_geom = jnp.clip(0.25 + 1.75 * jax.random.uniform(key_of[4], (2, S), jnp.float32) ** block_levels(key_of[4], (2, S), ((1, 16),), -0.2, 0.2), 0.25, 2.0)
    gust_index = place_ends(jax.random.randint(key_of[5], (G,), 0, NG), jax.random.fold_in(key_of[5], 1), 0, NG - 1).astype(jnp.int32)
    return dict(sym_press=sym_press, anti_press=anti_press, box_geom=box_geom, box_station=box_station, station_geom=station_geom, gust_index=gust_index)


def angle_table(count_a, count_b, length):
    product = (jnp.arange(count_a, dtype=jnp.int32)[:, None] * jnp.arange(count_b, dtype=jnp.int32)[None, :]) % length
    return product.astype(jnp.float32) * (2.0 * math.pi / length)


def gust_spectrum(gust_index, freqs, length):
    steps = jnp.arange(length, dtype=jnp.int32)
    samples = (gust_index + 8).astype(jnp.int32)
    phase = steps.astype(jnp.float32)[None, :] / samples.astype(jnp.float32)[:, None]
    profile = jnp.where(steps[None, :] < samples[:, None], 0.5 - 0.5 * jnp.cos(2.0 * math.pi * phase), 0.0)
    profile = profile.astype(jnp.float32)
    theta = angle_table(length, freqs, length)
    spec_re = jnp.dot(profile, jnp.cos(theta), precision=lax.Precision.HIGHEST)
    spec_im = -jnp.dot(profile, jnp.sin(theta), precision=lax.Precision.HIGHEST)
    return spec_re, spec_im


def weighted(press, geom):
    area = geom[0]
    weights = jnp.stack([area, area * geom[1], area * geom[2]])
    return (press[:, None] * weights[None, :, None, None, :]).astype(jnp.bfloat16)


def station_loads(cut, station_geom):
    cut_y = station_geom[0][:, None, None]
    cut_x = station_geom[1][:, None, None]

    def arms(part):
        shear = part[:, 0]
        return jnp.stack([shear, part[:, 1] - cut_y * shear, part[:, 2] - cut_x * shear], 1)

    left_part = arms(cut[:, 0])
    right_part = arms(cut[:, 1])
    return jnp.stack([left_part + right_part, left_part - right_part], 2)


def histories(loads, spec_re, spec_im, length):
    freqs = loads.shape[-1]
    load_re = loads[..., 0, :][..., None, :]
    load_im = loads[..., 1, :][..., None, :]
    resp_re = spec_re * load_re - spec_im * load_im
    resp_im = spec_re * load_im + spec_im * load_re
    response = jnp.concatenate([resp_re, resp_im], -1).astype(jnp.bfloat16)
    phi = angle_table(freqs, length, length)
    factor = (jnp.where(jnp.arange(freqs) == 0, 1.0, 2.0) / length).astype(jnp.float32)[:, None]
    basis = jnp.concatenate([factor * jnp.cos(phi), -factor * jnp.sin(phi)], 0).astype(jnp.bfloat16)
    flat = jnp.dot(response.reshape(-1, 2 * freqs), basis, preferred_element_type=jnp.float32)
    return flat.astype(jnp.bfloat16).reshape(response.shape[:-1] + (length,))


def reference(sym_press, anti_press, box_geom, box_station, station_geom, gust_index):
    anti = jnp.roll(anti_press, BOXES // 2, axis=2)
    terms = weighted(jnp.stack([sym_press, anti]), box_geom).reshape(12 * F, BOXES)
    strips = jax.ops.segment_sum(terms.astype(jnp.float32).T, box_station, num_segments=S)
    cut = jnp.flip(jnp.cumsum(jnp.flip(strips, 0), 0), 0).reshape(S, 2, 3, 2, F)
    loads = station_loads(cut, station_geom)
    spec_re, spec_im = gust_spectrum(gust_index, F, NFFT)
    return lax.map(lambda one: histories(one[None], spec_re, spec_im, NFFT)[0], loads)
```

```python
import math

import jax
import jax.numpy as jnp
import numpy as np
from jax import lax
from jax.sharding import PartitionSpec as P

NFFT = 512
FIRST_GUST = 8


def swap(block, axis, mask):
    count = lax.axis_size(axis)
    return lax.ppermute(block, axis, [(i, i ^ mask) for i in range(count)])


def fourier_rows(freqs, length):
    turns = np.arange(freqs)[:, None] * np.arange(length)[None, :] % length
    angle = turns * (2.0 * math.pi / length)
    return np.concatenate([np.cos(angle), -np.sin(angle)]).astype(np.float32)


def gust_spectrum(gust_index, rows):
    steps = jnp.arange(rows.shape[1], dtype=jnp.int32)
    samples = gust_index + FIRST_GUST
    phase = steps.astype(jnp.float32)[None, :] / samples.astype(jnp.float32)[:, None]
    profile = jnp.where(steps[None, :] < samples[:, None], 0.5 - 0.5 * jnp.cos(2.0 * math.pi * phase), 0.0)
    return lax.dot_general(profile, rows, (((1,), (1,)), ((), ())), precision=lax.Precision.HIGHEST)


def block_sums(press, geom, first, s_dev):
    area = geom[0]
    weights = jnp.stack([area, area * geom[1], area * geom[2]])
    ids = geom[3]
    marks = first + jnp.arange(s_dev, dtype=jnp.int32)
    masks = jnp.concatenate([jnp.ones_like(ids)[None], (ids[None] >= marks.astype(jnp.float32)[:, None]).astype(jnp.float32)])
    rows = (masks[:, None] * weights[None]).reshape(-1, weights.shape[1])
    flat = press.reshape(-1, press.shape[-1])
    sums = lax.dot_general(rows, flat, (((1,), (1,)), ((), ())), precision=lax.Precision.HIGHEST)
    return sums.reshape(1 + s_dev, 3, -1)


def on_device(sym_press, anti_press, box_geom, box_station, station_geom, gust_index):
    devices = lax.axis_size("box")
    me = lax.axis_index("box")
    half = devices // 2
    freqs = sym_press.shape[1]
    s_dev = station_geom.shape[1]

    geom = jnp.concatenate([box_geom, box_station.astype(jnp.float32)[None]])
    partner_geom = swap(geom, "box", half)
    sym = block_sums(sym_press, geom, me * s_dev, s_dev)
    anti = block_sums(anti_press, partner_geom, (me ^ half) * s_dev, s_dev)

    def later(mask, flip):
        return (((me ^ mask ^ flip) > (me ^ flip)).astype(jnp.float32))

    total = jnp.stack([sym[0], anti[0]])
    sym_part = sym[1:]
    anti_part = anti[1:]
    bits = devices.bit_length() - 1
    digits = []
    low = 0
    while low < bits:
        size = 2 if low + 2 <= bits else 1
        digits.append((low, size))
        low += size
    for low, size in digits[:-1]:
        masks = [v << low for v in range(1, 1 << size)]
        got = [swap(total, "box", mask) for mask in masks]
        for mask, part in zip(masks, got):
            sym_part = sym_part + later(mask, 0) * part[0]
            anti_part = anti_part + later(mask, half) * part[1]
        total = total + sum(got)
    low, size = digits[-1]
    masks = [v << low for v in range(1, 1 << size)]
    own_total = total
    home = swap(jnp.concatenate([anti_part, total[:1]]), "box", half)
    others = {mask: swap(total, "box", mask) for mask in masks if mask != half}
    anti_part = home[:-1] + later(half, 0) * own_total[1]
    sym_part = sym_part + later(half, 0) * home[-1]
    for mask, part in others.items():
        sym_part = sym_part + later(mask, 0) * part[0]
        anti_part = anti_part + later(mask ^ half, 0) * part[1]

    arm = station_geom[:, :, None]

    def arms(part):
        return jnp.stack([part[:, 0], part[:, 1] - arm[0] * part[:, 0], part[:, 2] - arm[1] * part[:, 0]], 1)

    left, right = arms(sym_part), arms(anti_part)
    loads = jnp.stack([left + right, left - right], 2)[..., None, :]
    rows = fourier_rows(freqs, NFFT)
    spec = gust_spectrum(gust_index, jnp.asarray(rows))
    spec_re, spec_im = spec[:, :freqs], spec[:, freqs:]
    load_re, load_im = loads[..., :freqs], loads[..., freqs:]
    response = jnp.concatenate(
        [spec_re * load_re - spec_im * load_im, spec_re * load_im + spec_im * load_re], -1
    ).astype(jnp.bfloat16)
    scale = np.where(np.arange(2 * freqs) % freqs == 0, 1.0, 2.0)[:, None] / NFFT
    basis = jnp.asarray((rows * scale).astype(np.float32)).astype(jnp.bfloat16)
    flat = jnp.dot(response.reshape(-1, 2 * freqs), basis, preferred_element_type=jnp.float32)
    return flat.astype(jnp.bfloat16).reshape(response.shape[:-1] + (NFFT,))


def solution(mesh):
    placed = (
        P("case", None, "box"),
        P("case", None, "box"),
        P(None, "box"),
        P("box"),
        P(None, "box"),
        P(),
    )
    return jax.shard_map(
        on_device,
        mesh=mesh,
        in_specs=placed,
        out_specs=P(("case", "box"), None, None, None, None),
        check_vma=False,
    )
```

```python
import math

import jax
import jax.numpy as jnp
import numpy as np
from jax import lax
from jax.experimental import pallas as pl
from jax.experimental.pallas import tpu as pltpu
from jax.sharding import PartitionSpec as P

NFFT = 512
FIRST_GUST = 8
LANES = 128


def swap(block, axis, mask):
    count = lax.axis_size(axis)
    return lax.ppermute(block, axis, [(i, i ^ mask) for i in range(count)])


def in_vmem(array):
    return pltpu.with_memory_space_constraint(array, pltpu.VMEM)


def fourier_rows(freqs, length):
    turns = np.arange(freqs)[:, None] * np.arange(length)[None, :] % length
    angle = turns * (2.0 * math.pi / length)
    return np.concatenate([np.cos(angle), -np.sin(angle)]).astype(np.float32)


def block_sums(press, geom, marks):
    area = geom[0:1]
    out = []
    for moment in range(3):
        weight = area if moment == 0 else area * geom[moment : moment + 1]
        terms = (press * weight).astype(jnp.bfloat16)
        out.append(
            lax.dot_general(marks, terms, (((1,), (1,)), ((), ())), preferred_element_type=jnp.float32)
        )
    return out


def station_marks(ids, s_dev):
    row = ids
    step = lax.broadcasted_iota(jnp.int32, (8, row.shape[1]), 0).astype(jnp.float32)
    last = row[:, row.shape[1] - 1 :]
    passed = jnp.broadcast_to(row - last, step.shape) >= step - s_dev
    return jnp.where((step == 0) | passed, 1.0, 0.0).astype(jnp.bfloat16)


def pack_kernel(geom_ref, ids_ref, out_ref):
    ids = ids_ref[...].astype(jnp.float32)
    out_ref[0:3] = geom_ref[...]
    out_ref[3:4] = jnp.concatenate([ids[i : i + 1] for i in range(ids.shape[0])], 1)


def pack_kernel(geom_ref, ids_ref, out_ref):
    ids = ids_ref[...].astype(jnp.float32)
    out_ref[0:3] = geom_ref[...]
    out_ref[3:4] = jnp.concatenate([ids[i : i + 1] for i in range(ids.shape[0])], 1)


def sym_kernel(s_dev, sym_ref, anti_ref, geom_ref, total_ref, part_ref, held_ref):
    rows = held_ref.shape[0]
    held_ref[...] = anti_ref[...].reshape(held_ref.shape)
    geom = geom_ref[...]
    sums = block_sums(sym_ref[...].reshape(rows, -1), geom, station_marks(geom[3:4], s_dev))
    for moment in range(3):
        total_ref[moment : moment + 1] = sums[moment][0:1]
        for k in range(s_dev):
            part_ref[k, moment : moment + 1] = sums[moment][1 + k : 2 + k]


def anti_kernel(s_dev, geom_ref, held_ref, total_ref, part_ref):
    geom = geom_ref[...]
    sums = block_sums(held_ref[...], geom, station_marks(geom[3:4], s_dev))
    for moment in range(3):
        total_ref[moment : moment + 1] = sums[moment][0:1]
        for k in range(s_dev):
            part_ref[k, moment : moment + 1] = sums[moment][1 + k : 2 + k]


def spectrum_kernel(index_ref, rows_ref, arm_ref, after_ref, spec_ref, arms_ref):
    for row in range(2):
        for s in range(arms_ref.shape[1]):
            arms_ref[row, s : s + 1] = jnp.broadcast_to(arm_ref[row : row + 1, s : s + 1], (1, arms_ref.shape[2]))
    gusts, length = spec_ref.shape[0], rows_ref.shape[1]
    index = jnp.broadcast_to(index_ref[...], (gusts, gusts))
    diagonal = lax.broadcasted_iota(jnp.int32, (gusts, gusts), 0) == lax.broadcasted_iota(
        jnp.int32, (gusts, gusts), 1
    )
    samples = jnp.sum(jnp.where(diagonal, index, 0), 1, keepdims=True) + FIRST_GUST
    steps = lax.broadcasted_iota(jnp.int32, (gusts, length), 1)
    phase = steps.astype(jnp.float32) / samples.astype(jnp.float32)
    profile = jnp.where(steps < samples, 0.5 - 0.5 * jnp.cos(2.0 * math.pi * phase), 0.0)
    spec_ref[...] = lax.dot_general(
        profile, rows_ref[...], (((1,), (1,)), ((), ())),
        precision=lax.Precision.HIGHEST, preferred_element_type=jnp.float32,
    )


def history_kernel(sym_ref, anti_ref, arm_ref, spec_ref, basis_ref, out_ref, rows_ref, sems):
    gusts, wide = spec_ref.shape
    freqs = wide // 2
    s_dev = sym_ref.shape[0]
    spec = spec_ref[...]
    lane = lax.broadcasted_iota(jnp.int32, (1, wide), 1)
    crossed = jnp.where(lane < freqs, -1.0, 1.0) * pltpu.roll(spec, freqs, 1)

    def arms(ref, s):
        shear = ref[s, 0:1]
        return [
            shear,
            ref[s, 1:2] - arm_ref[0, s : s + 1] * shear,
            ref[s, 2:3] - arm_ref[1, s : s + 1] * shear,
        ]

    copies = []
    for s in range(s_dev):
        left, right = arms(sym_ref, s), arms(anti_ref, s)
        for comp in range(3):
            blocks = []
            for load in (left[comp] + right[comp], left[comp] - right[comp]):
                turned = pltpu.roll(load, freqs, 1)
                load_re = jnp.where(lane < freqs, load, turned)
                load_im = jnp.where(lane < freqs, turned, load)
                blocks.append((spec * load_re + crossed * load_im).astype(jnp.bfloat16))
            first = (s * 3 + comp) * 2 * gusts
            here = pl.ds(first, 2 * gusts)
            rows_ref[here] = jnp.dot(
                jnp.concatenate(blocks), basis_ref[...], preferred_element_type=jnp.float32
            ).astype(jnp.bfloat16)
            copy = pltpu.make_async_copy(rows_ref.at[here], out_ref.at[here], sems.at[s * 3 + comp])
            copy.start()
            copies.append(copy)
    for copy in copies:
        copy.wait()


def on_device(sym_press, anti_press, box_geom, box_station, station_geom, gust_index):
    devices = lax.axis_size("box")
    me = lax.axis_index("box")
    half = devices // 2
    freqs = sym_press.shape[1]
    box_dev = sym_press.shape[2]
    s_dev = station_geom.shape[1]
    gusts = gust_index.shape[0]
    wide = 2 * freqs
    f32 = jnp.float32

    ids = box_station.reshape(-1, LANES)
    geom = pl.pallas_call(pack_kernel, out_shape=pltpu.VMEM((4, box_dev), f32), name="pack")(box_geom, ids)
    partner_geom = swap(geom, "box", half)
    sym_total, sym_part, held = pl.pallas_call(
        lambda *refs: sym_kernel(s_dev, *refs),
        out_shape=(
            pltpu.VMEM((3, wide), f32),
            pltpu.VMEM((s_dev, 3, wide), f32),
            pltpu.VMEM((wide, box_dev), f32),
        ),
        name="sym_sums",
    )(sym_press, anti_press, in_vmem(geom))
    anti_total, anti_part = pl.pallas_call(
        lambda *refs: anti_kernel(s_dev, *refs), out_shape=(pltpu.VMEM((3, wide), f32),pltpu.VMEM((s_dev, 3, wide), f32)), name="anti_sums"
    )(in_vmem(partner_geom), in_vmem(held))

    rows = fourier_rows(freqs, NFFT)
    spec, arm = pl.pallas_call(
        spectrum_kernel, out_shape=(pltpu.VMEM((gusts, wide), f32), pltpu.VMEM((2, s_dev, wide), f32)), name="spectrum"
    )(gust_index.reshape(1, gusts), in_vmem(jnp.asarray(rows)), station_geom, in_vmem(anti_total))
    scale = np.where(np.arange(wide) % freqs == 0, 1.0, 2.0)[:, None] / NFFT
    basis = jnp.asarray((rows * scale).astype(np.float32).astype(jnp.bfloat16))


    sent = jnp.concatenate([jnp.stack([sym_total, anti_total]), anti_part])
    got = swap(sent, "box", half ^ 1)
    is_low = (me < half).astype(f32)
    past = jnp.stack([got[0], anti_total]) * is_low
    total = jnp.stack([sym_total, got[1]])
    past, spec, arm = lax.optimization_barrier((past, spec, arm))
    state = jnp.concatenate([past, total])

    def later(mask):
        return ((me ^ mask) > me).astype(f32)

    got = swap(jnp.concatenate([state, got[2:]]), "box", 1)
    sym_part = sym_part + later(1) * got[2]
    anti_part = got[4:] + later(1) * total[1]
    state = state + got[:4]
    low, high = 1, half.bit_length() - 1
    while low < high:
        size = min(2, high - low)
        masks = [v << low for v in range(1, 1 << size)]
        parts = [swap(state, "box", mask ^ 1) for mask in masks]
        for mask, part in zip(masks, parts):
            sym_part = sym_part + later(mask) * part[2]
            anti_part = anti_part + later(mask) * part[3]
        state = state + sum(parts)
        low += size
    sym_part = sym_part + state[0]
    anti_part = anti_part + state[1]

    out = pl.pallas_call(
        history_kernel,
        out_shape=jax.ShapeDtypeStruct((s_dev * 6 * gusts, NFFT), jnp.bfloat16),
        out_specs=pl.BlockSpec(memory_space=pl.ANY),
        scratch_shapes=[
            pltpu.VMEM((s_dev * 6 * gusts, NFFT), jnp.bfloat16),
            pltpu.SemaphoreType.DMA((s_dev * 3,)),
        ],
        name="histories",
    )(in_vmem(sym_part), in_vmem(anti_part), in_vmem(arm), in_vmem(spec), in_vmem(basis))
    return out.reshape(s_dev, 3, 2, gusts, NFFT)


def solution(mesh):
    placed = (
        P("case", None, "box"),
        P("case", None, "box"),
        P(None, "box"),
        P("box"),
        P(None, "box"),
        P(),
    )
    return jax.shard_map(
        on_device,
        mesh=mesh,
        in_specs=placed,
        out_specs=P(("case", "box"), None, None, None, None),
        check_vma=False,
    )
```

```python
import math

import jax
import jax.numpy as jnp
import numpy as np
from jax import lax
from jax.experimental import pallas as pl
from jax.experimental.pallas import tpu as pltpu
from jax.sharding import PartitionSpec as P

NFFT = 512
FIRST_GUST = 8
LANES = 128


def swap(block, axis, mask):
    count = lax.axis_size(axis)
    return lax.ppermute(block, axis, [(i, i ^ mask) for i in range(count)])


def in_vmem(array):
    return pltpu.with_memory_space_constraint(array, pltpu.VMEM)


def fourier_rows(freqs, length):
    turns = np.arange(freqs)[:, None] * np.arange(length)[None, :] % length
    angle = turns * (2.0 * math.pi / length)
    return np.concatenate([np.cos(angle), -np.sin(angle)]).astype(np.float32)


def block_sums(press, geom, marks):
    area = geom[0:1]
    out = []
    for moment in range(3):
        weight = area if moment == 0 else area * geom[moment : moment + 1]
        terms = (press * weight).astype(jnp.bfloat16)
        out.append(
            lax.dot_general(marks, terms, (((1,), (1,)), ((), ())), preferred_element_type=jnp.float32)
        )
    return out


def station_marks(ids, s_dev):
    row = ids
    step = lax.broadcasted_iota(jnp.int32, (8, row.shape[1]), 0).astype(jnp.float32)
    last = row[:, row.shape[1] - 1 :]
    passed = jnp.broadcast_to(row - last, step.shape) >= step - s_dev
    return jnp.where((step == 0) | passed, 1.0, 0.0).astype(jnp.bfloat16)


def pack_kernel(geom_ref, ids_ref, out_ref):
    ids = ids_ref[...].astype(jnp.float32)
    out_ref[0:3] = geom_ref[...]
    out_ref[3:4] = jnp.concatenate([ids[i : i + 1] for i in range(ids.shape[0])], 1)


def pack_kernel(geom_ref, ids_ref, out_ref):
    ids = ids_ref[...].astype(jnp.float32)
    out_ref[0:3] = geom_ref[...]
    out_ref[3:4] = jnp.concatenate([ids[i : i + 1] for i in range(ids.shape[0])], 1)


def pack_kernel(geom_ref, ids_ref, out_ref):
    ids = ids_ref[...].astype(jnp.float32)
    out_ref[0:3] = geom_ref[...]
    out_ref[3:4] = jnp.concatenate([ids[i : i + 1] for i in range(ids.shape[0])], 1)


def sym_kernel(s_dev, sym_ref, geom_ref, total_ref, part_ref):
    rows = 2 * sym_ref.shape[1]
    geom = geom_ref[...]
    sums = block_sums(sym_ref[...].reshape(rows, -1), geom, station_marks(geom[3:4], s_dev))
    for moment in range(3):
        total_ref[moment : moment + 1] = sums[moment][0:1]
        for k in range(s_dev):
            part_ref[k, moment : moment + 1] = sums[moment][1 + k : 2 + k]


def split_kernel(s_dev, geom_ref, weight_ref, marks_ref):
    geom = geom_ref[...]
    weight_ref[...] = jnp.concatenate([geom[0:1], geom[0:1] * geom[1:2], geom[0:1] * geom[2:3]])
    marks_ref[...] = station_marks(geom[3:4], s_dev)


def anti_kernel(s_dev, weight_ref, marks_ref, anti_ref, total_ref, part_ref):
    rows = 2 * anti_ref.shape[1]
    press = anti_ref[...].reshape(rows, -1)
    for moment in range(3):
        terms = (press * weight_ref[moment : moment + 1]).astype(jnp.bfloat16)
        sums = lax.dot_general(
            marks_ref[...], terms, (((1,), (1,)), ((), ())), preferred_element_type=jnp.float32
        )
        total_ref[moment : moment + 1] = sums[0:1]
        for k in range(s_dev):
            part_ref[k, moment : moment + 1] = sums[1 + k : 2 + k]


def spectrum_kernel(index_ref, rows_ref, arm_ref, after_ref, spec_ref, arms_ref):
    for row in range(2):
        for s in range(arms_ref.shape[1]):
            arms_ref[row, s : s + 1] = jnp.broadcast_to(arm_ref[row : row + 1, s : s + 1], (1, arms_ref.shape[2]))
    gusts, length = spec_ref.shape[0], rows_ref.shape[1]
    index = jnp.broadcast_to(index_ref[...], (gusts, gusts))
    diagonal = lax.broadcasted_iota(jnp.int32, (gusts, gusts), 0) == lax.broadcasted_iota(
        jnp.int32, (gusts, gusts), 1
    )
    samples = jnp.sum(jnp.where(diagonal, index, 0), 1, keepdims=True) + FIRST_GUST
    steps = lax.broadcasted_iota(jnp.int32, (gusts, length), 1)
    phase = steps.astype(jnp.float32) / samples.astype(jnp.float32)
    profile = jnp.where(steps < samples, 0.5 - 0.5 * jnp.cos(2.0 * math.pi * phase), 0.0)
    spec_ref[...] = lax.dot_general(
        profile, rows_ref[...], (((1,), (1,)), ((), ())),
        precision=lax.Precision.HIGHEST, preferred_element_type=jnp.float32,
    )


def history_kernel(sym_ref, anti_ref, arm_ref, spec_ref, basis_ref, out_ref, rows_ref, sems):
    gusts, wide = spec_ref.shape
    freqs = wide // 2
    s_dev = sym_ref.shape[0]
    spec = spec_ref[...]
    lane = lax.broadcasted_iota(jnp.int32, (1, wide), 1)
    crossed = jnp.where(lane < freqs, -1.0, 1.0) * pltpu.roll(spec, freqs, 1)

    def arms(ref, s):
        shear = ref[s, 0:1]
        return [
            shear,
            ref[s, 1:2] - arm_ref[0, s : s + 1] * shear,
            ref[s, 2:3] - arm_ref[1, s : s + 1] * shear,
        ]

    copies = []
    for s in range(s_dev):
        left, right = arms(sym_ref, s), arms(anti_ref, s)
        for comp in range(3):
            blocks = []
            for load in (left[comp] + right[comp], left[comp] - right[comp]):
                turned = pltpu.roll(load, freqs, 1)
                load_re = jnp.where(lane < freqs, load, turned)
                load_im = jnp.where(lane < freqs, turned, load)
                blocks.append((spec * load_re + crossed * load_im).astype(jnp.bfloat16))
            first = (s * 3 + comp) * 2 * gusts
            here = pl.ds(first, 2 * gusts)
            rows_ref[here] = jnp.dot(
                jnp.concatenate(blocks), basis_ref[...], preferred_element_type=jnp.float32
            ).astype(jnp.bfloat16)
            copy = pltpu.make_async_copy(rows_ref.at[here], out_ref.at[here], sems.at[s * 3 + comp])
            copy.start()
            copies.append(copy)
    for copy in copies:
        copy.wait()


def on_device(sym_press, anti_press, box_geom, box_station, station_geom, gust_index):
    devices = lax.axis_size("box")
    me = lax.axis_index("box")
    half = devices // 2
    freqs = sym_press.shape[1]
    box_dev = sym_press.shape[2]
    s_dev = station_geom.shape[1]
    gusts = gust_index.shape[0]
    wide = 2 * freqs
    f32 = jnp.float32

    ids = box_station.reshape(-1, LANES)
    geom = pl.pallas_call(pack_kernel, out_shape=pltpu.VMEM((4, box_dev), f32), name="pack")(box_geom, ids)
    far_geom = swap(geom, "box", half ^ 1)
    near_anti = swap(anti_press, "box", 1)
    sym_total, sym_part = pl.pallas_call(
        lambda *refs: sym_kernel(s_dev, *refs),
        out_shape=(pltpu.VMEM((3, wide), f32), pltpu.VMEM((s_dev, 3, wide), f32)),
        name="sym_sums",
    )(sym_press, in_vmem(geom))
    weight, marks = pl.pallas_call(
        lambda *refs: split_kernel(s_dev, *refs),
        out_shape=(pltpu.VMEM((3, box_dev), f32), pltpu.VMEM((8, box_dev), jnp.bfloat16)),
        name="weights",
    )(in_vmem(far_geom))
    anti_total, anti_part = pl.pallas_call(
        lambda *refs: anti_kernel(s_dev, *refs), out_shape=(pltpu.VMEM((3, wide), f32),pltpu.VMEM((s_dev, 3, wide), f32)), name="anti_sums"
    )(in_vmem(weight), in_vmem(marks), in_vmem(near_anti))

    rows = fourier_rows(freqs, NFFT)
    scale = np.where(np.arange(wide) % freqs == 0, 1.0, 2.0)[:, None] / NFFT
    basis = jnp.asarray((rows * scale).astype(np.float32).astype(jnp.bfloat16))


    sent = jnp.concatenate([jnp.stack([sym_total, anti_total]), anti_part])
    got = swap(sent, "box", half ^ 1)
    is_low = (me < half).astype(f32)
    past = jnp.stack([got[0], anti_total]) * is_low
    total = jnp.stack([sym_total, got[1]])
    state = jnp.concatenate([past, total])

    def later(mask):
        return ((me ^ mask) > me).astype(f32)

    anti_part = got[2:]
    got = swap(state, "box", 1)
    sym_part = sym_part + later(1) * got[2]
    anti_part = anti_part + later(1) * got[3]
    state = state + got
    spec, arm = pl.pallas_call(
        spectrum_kernel, out_shape=(pltpu.VMEM((gusts, wide), f32), pltpu.VMEM((2, s_dev, wide), f32)), name="spectrum"
    )(gust_index.reshape(1, gusts), in_vmem(jnp.asarray(rows)), station_geom, in_vmem(state))
    low, high = 1, half.bit_length() - 1
    while low < high:
        size = min(2, high - low)
        masks = [v << low for v in range(1, 1 << size)]
        parts = [swap(state, "box", mask ^ 1) for mask in masks]
        for mask, part in zip(masks, parts):
            sym_part = sym_part + later(mask) * part[2]
            anti_part = anti_part + later(mask) * part[3]
        state = state + sum(parts)
        low += size
    sym_part = sym_part + state[0]
    anti_part = anti_part + state[1]

    out = pl.pallas_call(
        history_kernel,
        out_shape=jax.ShapeDtypeStruct((s_dev * 6 * gusts, NFFT), jnp.bfloat16),
        out_specs=pl.BlockSpec(memory_space=pl.ANY),
        scratch_shapes=[
            pltpu.VMEM((s_dev * 6 * gusts, NFFT), jnp.bfloat16),
            pltpu.SemaphoreType.DMA((s_dev * 3,)),
        ],
        name="histories",
    )(in_vmem(sym_part), in_vmem(anti_part), in_vmem(arm), in_vmem(spec), in_vmem(basis))
    return out.reshape(s_dev, 3, 2, gusts, NFFT)


def solution(mesh):
    placed = (
        P("case", None, "box"),
        P("case", None, "box"),
        P(None, "box"),
        P("box"),
        P(None, "box"),
        P(),
    )
    return jax.shard_map(
        on_device,
        mesh=mesh,
        in_specs=placed,
        out_specs=P(("case", "box"), None, None, None, None),
        check_vma=False,
    )
```

```python
import math

import jax
import jax.numpy as jnp
import numpy as np
from jax import lax
from jax.experimental import pallas as pl
from jax.experimental.pallas import tpu as pltpu
from jax.sharding import PartitionSpec as P

NFFT = 512
FIRST_GUST = 8
LANES = 128


def swap(block, axis, mask):
    count = lax.axis_size(axis)
    return lax.ppermute(block, axis, [(i, i ^ mask) for i in range(count)])


def in_vmem(array):
    return pltpu.with_memory_space_constraint(array, pltpu.VMEM)


def fourier_rows(freqs, length):
    turns = np.arange(freqs)[:, None] * np.arange(length)[None, :] % length
    angle = turns * (2.0 * math.pi / length)
    return np.concatenate([np.cos(angle), -np.sin(angle)]).astype(np.float32)


def block_sums(press, geom, marks):
    area = geom[0:1]
    out = []
    for moment in range(3):
        weight = area if moment == 0 else area * geom[moment : moment + 1]
        terms = (press * weight).astype(jnp.bfloat16)
        out.append(
            lax.dot_general(marks, terms, (((1,), (1,)), ((), ())), preferred_element_type=jnp.float32)
        )
    return out


def station_marks(ids, s_dev):
    row = ids
    step = lax.broadcasted_iota(jnp.int32, (8, row.shape[1]), 0).astype(jnp.float32)
    last = row[:, row.shape[1] - 1 :]
    passed = jnp.broadcast_to(row - last, step.shape) >= step - s_dev
    return jnp.where((step == 0) | passed, 1.0, 0.0).astype(jnp.bfloat16)


def pack_kernel(geom_ref, ids_ref, out_ref):
    ids = ids_ref[...].astype(jnp.float32)
    out_ref[0:3] = geom_ref[...]
    out_ref[3:4] = jnp.concatenate([ids[i : i + 1] for i in range(ids.shape[0])], 1)


def pack_kernel(geom_ref, ids_ref, out_ref):
    ids = ids_ref[...].astype(jnp.float32)
    out_ref[0:3] = geom_ref[...]
    out_ref[3:4] = jnp.concatenate([ids[i : i + 1] for i in range(ids.shape[0])], 1)


def pack_kernel(geom_ref, ids_ref, out_ref):
    ids = ids_ref[...].astype(jnp.float32)
    out_ref[0:3] = geom_ref[...]
    out_ref[3:4] = jnp.concatenate([ids[i : i + 1] for i in range(ids.shape[0])], 1)


def sym_kernel(s_dev, sym_ref, geom_ref, total_ref, part_ref):
    rows = 2 * sym_ref.shape[1]
    geom = geom_ref[...]
    sums = block_sums(sym_ref[...].reshape(rows, -1), geom, station_marks(geom[3:4], s_dev))
    for moment in range(3):
        total_ref[moment : moment + 1] = sums[moment][0:1]
        for k in range(s_dev):
            part_ref[k, moment : moment + 1] = sums[moment][1 + k : 2 + k]


def anti_kernel(s_dev, geom_ref, anti_ref, sym_ref, sent_ref):
    geom = geom_ref[...]
    rows = 2 * anti_ref.shape[1]
    sums = block_sums(anti_ref[...].reshape(rows, -1), geom, station_marks(geom[3:4], s_dev))
    sent_ref[0] = sym_ref[...]
    for moment in range(3):
        for k in range(1 + s_dev):
            sent_ref[1 + k, moment : moment + 1] = sums[moment][k : k + 1]


def spectrum_kernel(index_ref, rows_ref, arm_ref, after_ref, spec_ref, arms_ref):
    for row in range(2):
        for s in range(arms_ref.shape[1]):
            arms_ref[row, s : s + 1] = jnp.broadcast_to(arm_ref[row : row + 1, s : s + 1], (1, arms_ref.shape[2]))
    gusts, length = spec_ref.shape[0], rows_ref.shape[1]
    index = jnp.broadcast_to(index_ref[...], (gusts, gusts))
    diagonal = lax.broadcasted_iota(jnp.int32, (gusts, gusts), 0) == lax.broadcasted_iota(
        jnp.int32, (gusts, gusts), 1
    )
    samples = jnp.sum(jnp.where(diagonal, index, 0), 1, keepdims=True) + FIRST_GUST
    steps = lax.broadcasted_iota(jnp.int32, (gusts, length), 1)
    phase = steps.astype(jnp.float32) / samples.astype(jnp.float32)
    profile = jnp.where(steps < samples, 0.5 - 0.5 * jnp.cos(2.0 * math.pi * phase), 0.0)
    spec_ref[...] = lax.dot_general(
        profile, rows_ref[...], (((1,), (1,)), ((), ())),
        precision=lax.Precision.HIGHEST, preferred_element_type=jnp.float32,
    )


def history_kernel(sym_ref, anti_ref, arm_ref, spec_ref, basis_ref, out_ref, rows_ref, sems):
    gusts, wide = spec_ref.shape
    freqs = wide // 2
    s_dev = sym_ref.shape[0]
    spec = spec_ref[...]
    lane = lax.broadcasted_iota(jnp.int32, (1, wide), 1)
    crossed = jnp.where(lane < freqs, -1.0, 1.0) * pltpu.roll(spec, freqs, 1)

    def arms(ref, s):
        shear = ref[s, 0:1]
        return [
            shear,
            ref[s, 1:2] - arm_ref[0, s : s + 1] * shear,
            ref[s, 2:3] - arm_ref[1, s : s + 1] * shear,
        ]

    copies = []
    for s in range(s_dev):
        left, right = arms(sym_ref, s), arms(anti_ref, s)
        for comp in range(3):
            blocks = []
            for load in (left[comp] + right[comp], left[comp] - right[comp]):
                turned = pltpu.roll(load, freqs, 1)
                load_re = jnp.where(lane < freqs, load, turned)
                load_im = jnp.where(lane < freqs, turned, load)
                blocks.append((spec * load_re + crossed * load_im).astype(jnp.bfloat16))
            first = (s * 3 + comp) * 2 * gusts
            here = pl.ds(first, 2 * gusts)
            rows_ref[here] = jnp.dot(
                jnp.concatenate(blocks), basis_ref[...], preferred_element_type=jnp.float32
            ).astype(jnp.bfloat16)
            copy = pltpu.make_async_copy(rows_ref.at[here], out_ref.at[here], sems.at[s * 3 + comp])
            copy.start()
            copies.append(copy)
    for copy in copies:
        copy.wait()


def on_device(sym_press, anti_press, box_geom, box_station, station_geom, gust_index):
    devices = lax.axis_size("box")
    me = lax.axis_index("box")
    half = devices // 2
    freqs = sym_press.shape[1]
    box_dev = sym_press.shape[2]
    s_dev = station_geom.shape[1]
    gusts = gust_index.shape[0]
    wide = 2 * freqs
    f32 = jnp.float32

    ids = box_station.reshape(-1, LANES)
    geom = pl.pallas_call(pack_kernel, out_shape=pltpu.VMEM((4, box_dev), f32), name="pack")(box_geom, ids)
    far_geom = swap(geom, "box", half ^ 1)
    near_anti = swap(anti_press, "box", 1)
    sym_total, sym_part = pl.pallas_call(
        lambda *refs: sym_kernel(s_dev, *refs),
        out_shape=(pltpu.VMEM((3, wide), f32), pltpu.VMEM((s_dev, 3, wide), f32)),
        name="sym_sums",
    )(sym_press, in_vmem(geom))
    sent = pl.pallas_call(
        lambda *refs: anti_kernel(s_dev, *refs),
        out_shape=pltpu.VMEM((2 + s_dev, 3, wide), f32),
        name="anti_sums",
    )(in_vmem(far_geom), in_vmem(near_anti), in_vmem(sym_total))

    rows = fourier_rows(freqs, NFFT)
    scale = np.where(np.arange(wide) % freqs == 0, 1.0, 2.0)[:, None] / NFFT
    basis = jnp.asarray((rows * scale).astype(np.float32).astype(jnp.bfloat16))


    got = swap(sent, "box", half ^ 1)
    is_low = (me < half).astype(f32)
    past = jnp.stack([got[0], sent[1]]) * is_low
    total = jnp.stack([sym_total, got[1]])
    state = jnp.concatenate([past, total])

    def later(mask):
        return ((me ^ mask) > me).astype(f32)

    anti_part = got[2:]
    got = swap(state, "box", 1)
    sym_part = sym_part + later(1) * got[2]
    anti_part = anti_part + later(1) * got[3]
    state = state + got
    spec, arm = pl.pallas_call(
        spectrum_kernel, out_shape=(pltpu.VMEM((gusts, wide), f32), pltpu.VMEM((2, s_dev, wide), f32)), name="spectrum"
    )(gust_index.reshape(1, gusts), in_vmem(jnp.asarray(rows)), station_geom, in_vmem(state))
    low, high = 1, half.bit_length() - 1
    while low < high:
        size = min(2, high - low)
        masks = [v << low for v in range(1, 1 << size)]
        parts = [swap(state, "box", mask ^ 1) for mask in masks]
        for mask, part in zip(masks, parts):
            sym_part = sym_part + later(mask) * part[2]
            anti_part = anti_part + later(mask) * part[3]
        state = state + sum(parts)
        low += size
    sym_part = sym_part + state[0]
    anti_part = anti_part + state[1]

    out = pl.pallas_call(
        history_kernel,
        out_shape=jax.ShapeDtypeStruct((s_dev * 6 * gusts, NFFT), jnp.bfloat16),
        out_specs=pl.BlockSpec(memory_space=pl.ANY),
        scratch_shapes=[
            pltpu.VMEM((s_dev * 6 * gusts, NFFT), jnp.bfloat16),
            pltpu.SemaphoreType.DMA((s_dev * 3,)),
        ],
        name="histories",
    )(in_vmem(sym_part), in_vmem(anti_part), in_vmem(arm), in_vmem(spec), in_vmem(basis))
    return out.reshape(s_dev, 3, 2, gusts, NFFT)


def solution(mesh):
    placed = (
        P("case", None, "box"),
        P("case", None, "box"),
        P(None, "box"),
        P("box"),
        P(None, "box"),
        P(),
    )
    return jax.shard_map(
        on_device,
        mesh=mesh,
        in_specs=placed,
        out_specs=P(("case", "box"), None, None, None, None),
        check_vma=False,
    )
```

```python
import math

import jax
import jax.numpy as jnp
import numpy as np
from jax import lax
from jax.experimental import pallas as pl
from jax.experimental.pallas import tpu as pltpu
from jax.sharding import PartitionSpec as P

NFFT = 512
FIRST_GUST = 8
LANES = 128


def swap(block, axis, mask):
    count = lax.axis_size(axis)
    return lax.ppermute(block, axis, [(i, i ^ mask) for i in range(count)])


def in_vmem(array):
    return pltpu.with_memory_space_constraint(array, pltpu.VMEM)


def fourier_rows(freqs, length):
    turns = np.arange(freqs)[:, None] * np.arange(length)[None, :] % length
    angle = turns * (2.0 * math.pi / length)
    return np.concatenate([np.cos(angle), -np.sin(angle)]).astype(np.float32)


def block_sums(press, geom, marks):
    area = geom[0:1]
    out = []
    for moment in range(3):
        weight = area if moment == 0 else area * geom[moment : moment + 1]
        terms = (press * weight).astype(jnp.bfloat16)
        out.append(
            lax.dot_general(marks, terms, (((1,), (1,)), ((), ())), preferred_element_type=jnp.float32)
        )
    return out


def station_marks(ids, s_dev):
    row = ids
    step = lax.broadcasted_iota(jnp.int32, (8, row.shape[1]), 0).astype(jnp.float32)
    last = row[:, row.shape[1] - 1 :]
    passed = jnp.broadcast_to(row - last, step.shape) >= step - s_dev
    return jnp.where((step == 0) | passed, 1.0, 0.0).astype(jnp.bfloat16)


def pack_kernel(geom_ref, ids_ref, out_ref):
    ids = ids_ref[...].astype(jnp.float32)
    out_ref[0:3] = geom_ref[...]
    out_ref[3:4] = jnp.concatenate([ids[i : i + 1] for i in range(ids.shape[0])], 1)


def pack_kernel(geom_ref, ids_ref, out_ref):
    ids = ids_ref[...].astype(jnp.float32)
    out_ref[0:3] = geom_ref[...]
    out_ref[3:4] = jnp.concatenate([ids[i : i + 1] for i in range(ids.shape[0])], 1)


def pack_kernel(geom_ref, ids_ref, out_ref):
    ids = ids_ref[...].astype(jnp.float32)
    out_ref[0:3] = geom_ref[...]
    out_ref[3:4] = jnp.concatenate([ids[i : i + 1] for i in range(ids.shape[0])], 1)


def sym_kernel(s_dev, sym_ref, geom_ref, total_ref, part_ref):
    rows = 2 * sym_ref.shape[1]
    geom = geom_ref[...]
    sums = block_sums(sym_ref[...].reshape(rows, -1), geom, station_marks(geom[3:4], s_dev))
    for moment in range(3):
        total_ref[moment : moment + 1] = sums[moment][0:1]
        for k in range(s_dev):
            part_ref[k, moment : moment + 1] = sums[moment][1 + k : 2 + k]


def anti_kernel(s_dev, geom_ref, anti_ref, sym_ref, sent_ref):
    geom = geom_ref[...]
    rows = 2 * anti_ref.shape[1]
    sums = block_sums(anti_ref[...].reshape(rows, -1), geom, station_marks(geom[3:4], s_dev))
    sent_ref[0] = sym_ref[...]
    for moment in range(3):
        for k in range(1 + s_dev):
            sent_ref[1 + k, moment : moment + 1] = sums[moment][k : k + 1]


def spectrum_kernel(index_ref, rows_ref, arm_ref, after_ref, spec_ref, arms_ref):
    for row in range(2):
        for s in range(arms_ref.shape[1]):
            arms_ref[row, s : s + 1] = jnp.broadcast_to(arm_ref[row : row + 1, s : s + 1], (1, arms_ref.shape[2]))
    gusts, length = spec_ref.shape[0], rows_ref.shape[1]
    index = jnp.broadcast_to(index_ref[...], (gusts, gusts))
    diagonal = lax.broadcasted_iota(jnp.int32, (gusts, gusts), 0) == lax.broadcasted_iota(
        jnp.int32, (gusts, gusts), 1
    )
    samples = jnp.sum(jnp.where(diagonal, index, 0), 1, keepdims=True) + FIRST_GUST
    steps = lax.broadcasted_iota(jnp.int32, (gusts, length), 1)
    phase = steps.astype(jnp.float32) / samples.astype(jnp.float32)
    profile = jnp.where(steps < samples, 0.5 - 0.5 * jnp.cos(2.0 * math.pi * phase), 0.0)
    spec_ref[...] = lax.dot_general(
        profile, rows_ref[...], (((1,), (1,)), ((), ())),
        precision=lax.Precision.HIGHEST, preferred_element_type=jnp.float32,
    )


def history_kernel(sym_ref, anti_ref, arm_ref, spec_ref, basis_ref, out_ref, rows_ref, sems):
    gusts, wide = spec_ref.shape
    freqs = wide // 2
    s_dev = sym_ref.shape[0]
    spec = spec_ref[...]
    lane = lax.broadcasted_iota(jnp.int32, (1, wide), 1)
    crossed = jnp.where(lane < freqs, -1.0, 1.0) * pltpu.roll(spec, freqs, 1)

    def arms(ref, s):
        shear = ref[s, 0:1]
        return [
            shear,
            ref[s, 1:2] - arm_ref[0, s : s + 1] * shear,
            ref[s, 2:3] - arm_ref[1, s : s + 1] * shear,
        ]

    copies = []
    for s in range(s_dev):
        left, right = arms(sym_ref, s), arms(anti_ref, s)
        for comp in range(3):
            blocks = []
            for load in (left[comp] + right[comp], left[comp] - right[comp]):
                turned = pltpu.roll(load, freqs, 1)
                load_re = jnp.where(lane < freqs, load, turned)
                load_im = jnp.where(lane < freqs, turned, load)
                blocks.append((spec * load_re + crossed * load_im).astype(jnp.bfloat16))
            first = (s * 3 + comp) * 2 * gusts
            here = pl.ds(first, 2 * gusts)
            rows_ref[here] = jnp.dot(
                jnp.concatenate(blocks), basis_ref[...], preferred_element_type=jnp.float32
            ).astype(jnp.bfloat16)
            copy = pltpu.make_async_copy(rows_ref.at[here], out_ref.at[here], sems.at[s * 3 + comp])
            copy.start()
            copies.append(copy)
    for copy in copies:
        copy.wait()


def on_device(sym_press, anti_press, box_geom, box_station, station_geom, gust_index):
    devices = lax.axis_size("box")
    me = lax.axis_index("box")
    half = devices // 2
    freqs = sym_press.shape[1]
    box_dev = sym_press.shape[2]
    s_dev = station_geom.shape[1]
    gusts = gust_index.shape[0]
    wide = 2 * freqs
    f32 = jnp.float32

    ids = box_station.reshape(-1, LANES)
    geom = pl.pallas_call(pack_kernel, out_shape=pltpu.VMEM((4, box_dev), f32), name="pack")(box_geom, ids)
    far_geom = swap(geom, "box", half ^ 1)
    near_anti = swap(anti_press, "box", 1)
    sym_total, sym_part = pl.pallas_call(
        lambda *refs: sym_kernel(s_dev, *refs),
        out_shape=(pltpu.VMEM((3, wide), f32), pltpu.VMEM((s_dev, 3, wide), f32)),
        name="sym_sums",
    )(sym_press, in_vmem(geom))
    sent = pl.pallas_call(
        lambda *refs: anti_kernel(s_dev, *refs),
        out_shape=pltpu.VMEM((2 + s_dev, 3, wide), f32),
        name="anti_sums",
    )(in_vmem(far_geom), in_vmem(near_anti), in_vmem(sym_total))

    rows = fourier_rows(freqs, NFFT)
    scale = np.where(np.arange(wide) % freqs == 0, 1.0, 2.0)[:, None] / NFFT
    basis = jnp.asarray((rows * scale).astype(np.float32).astype(jnp.bfloat16))


    def later(mask):
        return ((me ^ mask) > me).astype(f32)

    total, anti_part = sent[:2], sent[2:]
    got = swap(total, "box", 1)
    sym_part = sym_part + later(1) * got[0]
    anti_part = anti_part + (1.0 - later(1)) * got[1]
    total = total + got
    spec, arm = pl.pallas_call(
        spectrum_kernel, out_shape=(pltpu.VMEM((gusts, wide), f32), pltpu.VMEM((2, s_dev, wide), f32)), name="spectrum"
    )(gust_index.reshape(1, gusts), in_vmem(jnp.asarray(rows)), station_geom, in_vmem(total))
    low, high = 1, half.bit_length() - 1
    while low < high:
        size = min(2, high - low)
        masks = [v << low for v in range(1, 1 << size)]
        parts = [swap(total, "box", mask ^ 1) for mask in masks]
        for mask, part in zip(masks, parts):
            sym_part = sym_part + later(mask) * part[0]
            anti_part = anti_part + later(mask) * part[1]
        total = total + sum(parts)
        low += size
    is_low = (me < half).astype(f32)
    anti_part, spec, arm = lax.optimization_barrier((anti_part, spec, arm))
    got = swap(jnp.concatenate([anti_part, total[:1]]), "box", half ^ 1)
    anti_part = got[:-1] + is_low * total[1]
    sym_part = sym_part + is_low * got[-1]

    out = pl.pallas_call(
        history_kernel,
        out_shape=jax.ShapeDtypeStruct((s_dev * 6 * gusts, NFFT), jnp.bfloat16),
        out_specs=pl.BlockSpec(memory_space=pl.ANY),
        scratch_shapes=[
            pltpu.VMEM((s_dev * 6 * gusts, NFFT), jnp.bfloat16),
            pltpu.SemaphoreType.DMA((s_dev * 3,)),
        ],
        name="histories",
    )(in_vmem(sym_part), in_vmem(anti_part), in_vmem(arm), in_vmem(spec), in_vmem(basis))
    return out.reshape(s_dev, 3, 2, gusts, NFFT)


def solution(mesh):
    placed = (
        P("case", None, "box"),
        P("case", None, "box"),
        P(None, "box"),
        P("box"),
        P(None, "box"),
        P(),
    )
    return jax.shard_map(
        on_device,
        mesh=mesh,
        in_specs=placed,
        out_specs=P(("case", "box"), None, None, None, None),
        check_vma=False,
    )
```

```python
import math

import jax
import jax.numpy as jnp
import numpy as np
from jax import lax
from jax.experimental import pallas as pl
from jax.experimental.pallas import tpu as pltpu
from jax.sharding import PartitionSpec as P

NFFT = 512
FIRST_GUST = 8
LANES = 128


def swap(block, axis, mask):
    count = lax.axis_size(axis)
    return lax.ppermute(block, axis, [(i, i ^ mask) for i in range(count)])


def in_vmem(array):
    return pltpu.with_memory_space_constraint(array, pltpu.VMEM)


def fourier_rows(freqs, length):
    turns = np.arange(freqs)[:, None] * np.arange(length)[None, :] % length
    angle = turns * (2.0 * math.pi / length)
    return np.concatenate([np.cos(angle), -np.sin(angle)]).astype(np.float32)


def block_sums(press, geom, marks):
    area = geom[0:1]
    out = []
    for moment in range(3):
        weight = area if moment == 0 else area * geom[moment : moment + 1]
        terms = (press * weight).astype(jnp.bfloat16)
        out.append(
            lax.dot_general(marks, terms, (((1,), (1,)), ((), ())), preferred_element_type=jnp.float32)
        )
    return out


def station_marks(ids, s_dev):
    row = ids
    step = lax.broadcasted_iota(jnp.int32, (8, row.shape[1]), 0).astype(jnp.float32)
    last = row[:, row.shape[1] - 1 :]
    passed = jnp.broadcast_to(row - last, step.shape) >= step - s_dev
    return jnp.where((step == 0) | passed, 1.0, 0.0).astype(jnp.bfloat16)


def pack_kernel(geom_ref, ids_ref, out_ref):
    ids = ids_ref[...].astype(jnp.float32)
    out_ref[0:3] = geom_ref[...]
    out_ref[3:4] = jnp.concatenate([ids[i : i + 1] for i in range(ids.shape[0])], 1)


def sym_kernel(s_dev, sym_ref, geom_ref, total_ref, part_ref):
    rows = 2 * sym_ref.shape[1]
    geom = geom_ref[...]
    sums = block_sums(sym_ref[...].reshape(rows, -1), geom, station_marks(geom[3:4], s_dev))
    for moment in range(3):
        total_ref[moment : moment + 1] = sums[moment][0:1]
        for k in range(s_dev):
            part_ref[k, moment : moment + 1] = sums[moment][1 + k : 2 + k]


def anti_kernel(s_dev, geom_ref, anti_ref, sym_ref, sent_ref):
    geom = geom_ref[...]
    rows = 2 * anti_ref.shape[1]
    sums = block_sums(anti_ref[...].reshape(rows, -1), geom, station_marks(geom[3:4], s_dev))
    sent_ref[0] = sym_ref[...]
    for moment in range(3):
        for k in range(1 + s_dev):
            sent_ref[1 + k, moment : moment + 1] = sums[moment][k : k + 1]


def spectrum_kernel(index_ref, rows_ref, arm_ref, after_ref, spec_ref, arms_ref):
    for row in range(2):
        for s in range(arms_ref.shape[1]):
            arms_ref[row, s : s + 1] = jnp.broadcast_to(arm_ref[row : row + 1, s : s + 1], (1, arms_ref.shape[2]))
    gusts, length = spec_ref.shape[0], rows_ref.shape[1]
    index = jnp.broadcast_to(index_ref[...], (gusts, gusts))
    diagonal = lax.broadcasted_iota(jnp.int32, (gusts, gusts), 0) == lax.broadcasted_iota(
        jnp.int32, (gusts, gusts), 1
    )
    samples = jnp.sum(jnp.where(diagonal, index, 0), 1, keepdims=True) + FIRST_GUST
    steps = lax.broadcasted_iota(jnp.int32, (gusts, length), 1)
    phase = steps.astype(jnp.float32) / samples.astype(jnp.float32)
    profile = jnp.where(steps < samples, 0.5 - 0.5 * jnp.cos(2.0 * math.pi * phase), 0.0)
    spec_ref[...] = lax.dot_general(
        profile, rows_ref[...], (((1,), (1,)), ((), ())),
        precision=lax.Precision.HIGHEST, preferred_element_type=jnp.float32,
    )


def history_kernel(sym_ref, anti_ref, arm_ref, spec_ref, basis_ref, out_ref, rows_ref, sems):
    gusts, wide = spec_ref.shape
    freqs = wide // 2
    s_dev = sym_ref.shape[0]
    spec = spec_ref[...]
    lane = lax.broadcasted_iota(jnp.int32, (1, wide), 1)
    crossed = jnp.where(lane < freqs, -1.0, 1.0) * pltpu.roll(spec, freqs, 1)

    def arms(ref, s):
        shear = ref[s, 0:1]
        return [
            shear,
            ref[s, 1:2] - arm_ref[0, s : s + 1] * shear,
            ref[s, 2:3] - arm_ref[1, s : s + 1] * shear,
        ]

    copies = []
    for s in range(s_dev):
        left, right = arms(sym_ref, s), arms(anti_ref, s)
        for comp in range(3):
            blocks = []
            for load in (left[comp] + right[comp], left[comp] - right[comp]):
                turned = pltpu.roll(load, freqs, 1)
                load_re = jnp.where(lane < freqs, load, turned)
                load_im = jnp.where(lane < freqs, turned, load)
                blocks.append((spec * load_re + crossed * load_im).astype(jnp.bfloat16))
            first = (s * 3 + comp) * 2 * gusts
            here = pl.ds(first, 2 * gusts)
            rows_ref[here] = jnp.dot(
                jnp.concatenate(blocks), basis_ref[...], preferred_element_type=jnp.float32
            ).astype(jnp.bfloat16)
            copy = pltpu.make_async_copy(rows_ref.at[here], out_ref.at[here], sems.at[s * 3 + comp])
            copy.start()
            copies.append(copy)
    for copy in copies:
        copy.wait()


def on_device(sym_press, anti_press, box_geom, box_station, station_geom, gust_index):
    devices = lax.axis_size("box")
    me = lax.axis_index("box")
    half = devices // 2
    freqs = sym_press.shape[1]
    box_dev = sym_press.shape[2]
    s_dev = station_geom.shape[1]
    gusts = gust_index.shape[0]
    wide = 2 * freqs
    f32 = jnp.float32

    ids = box_station.reshape(-1, LANES)
    geom = pl.pallas_call(pack_kernel, out_shape=pltpu.VMEM((4, box_dev), f32), name="pack")(box_geom, ids)
    far_geom = swap(geom, "box", half ^ 1)
    near_anti = swap(anti_press, "box", 1)
    sym_total, sym_part = pl.pallas_call(
        lambda *refs: sym_kernel(s_dev, *refs),
        out_shape=(pltpu.VMEM((3, wide), f32), pltpu.VMEM((s_dev, 3, wide), f32)),
        name="sym_sums",
    )(sym_press, in_vmem(geom))
    sent = pl.pallas_call(
        lambda *refs: anti_kernel(s_dev, *refs),
        out_shape=pltpu.VMEM((2 + s_dev, 3, wide), f32),
        name="anti_sums",
    )(in_vmem(far_geom), in_vmem(near_anti), in_vmem(sym_total))

    rows = fourier_rows(freqs, NFFT)
    scale = np.where(np.arange(wide) % freqs == 0, 1.0, 2.0)[:, None] / NFFT
    basis = jnp.asarray((rows * scale).astype(np.float32).astype(jnp.bfloat16))

    def later(mask):
        return ((me ^ mask) > me).astype(f32)

    total, anti_part = sent[:2], sent[2:]
    got = swap(total, "box", 1)
    sym_part = sym_part + later(1) * got[0]
    anti_part = anti_part + (1.0 - later(1)) * got[1]
    total = total + got
    spec, arm = pl.pallas_call(
        spectrum_kernel, out_shape=(pltpu.VMEM((gusts, wide), f32), pltpu.VMEM((2, s_dev, wide), f32)), name="spectrum"
    )(gust_index.reshape(1, gusts), in_vmem(jnp.asarray(rows)), station_geom, in_vmem(total))
    low, high = 1, half.bit_length() - 1
    while low < high:
        size = min(2, high - low)
        masks = [v << low for v in range(1, 1 << size)]
        parts = [swap(total, "box", mask ^ 1) for mask in masks]
        for mask, part in zip(masks, parts):
            sym_part = sym_part + later(mask) * part[0]
            anti_part = anti_part + later(mask) * part[1]
        total = total + sum(parts)
        low += size
    is_low = (me < half).astype(f32)
    anti_part, spec, arm = lax.optimization_barrier((anti_part, spec, arm))
    got = swap(jnp.concatenate([anti_part, total[:1]]), "box", half ^ 1)
    anti_part = got[:-1] + is_low * total[1]
    sym_part = sym_part + is_low * got[-1]

    out = pl.pallas_call(
        history_kernel,
        out_shape=jax.ShapeDtypeStruct((s_dev * 6 * gusts, NFFT), jnp.bfloat16),
        out_specs=pl.BlockSpec(memory_space=pl.ANY),
        scratch_shapes=[
            pltpu.VMEM((s_dev * 6 * gusts, NFFT), jnp.bfloat16),
            pltpu.SemaphoreType.DMA((s_dev * 3,)),
        ],
        name="histories",
    )(in_vmem(sym_part), in_vmem(anti_part), in_vmem(arm), in_vmem(spec), in_vmem(basis))
    return out.reshape(s_dev, 3, 2, gusts, NFFT)


def solution(mesh):
    placed = (
        P("case", None, "box"),
        P("case", None, "box"),
        P(None, "box"),
        P("box"),
        P(None, "box"),
        P(),
    )
    return jax.shard_map(
        on_device,
        mesh=mesh,
        in_specs=placed,
        out_specs=P(("case", "box"), None, None, None, None),
        check_vma=False,
    )
```

```python
import math

import jax
import jax.numpy as jnp
import numpy as np
from jax import lax
from jax.experimental import pallas as pl
from jax.experimental.pallas import tpu as pltpu
from jax.sharding import PartitionSpec as P

NFFT = 512
FIRST_GUST = 8
LANES = 128


def swap(block, axis, mask):
    count = lax.axis_size(axis)
    return lax.ppermute(block, axis, [(i, i ^ mask) for i in range(count)])


def in_vmem(array):
    return pltpu.with_memory_space_constraint(array, pltpu.VMEM)


def fourier_rows(freqs, length):
    turns = np.arange(freqs)[:, None] * np.arange(length)[None, :] % length
    angle = turns * (2.0 * math.pi / length)
    return np.concatenate([np.cos(angle), -np.sin(angle)]).astype(np.float32)


def block_sums(press, geom, marks):
    area = geom[0:1]
    out = []
    for moment in range(3):
        weight = area if moment == 0 else area * geom[moment : moment + 1]
        terms = (press * weight).astype(jnp.bfloat16)
        out.append(
            lax.dot_general(marks, terms, (((1,), (1,)), ((), ())), preferred_element_type=jnp.float32)
        )
    return out


def station_marks(ids, s_dev):
    row = ids
    step = lax.broadcasted_iota(jnp.int32, (8, row.shape[1]), 0).astype(jnp.float32)
    last = row[:, row.shape[1] - 1 :]
    passed = jnp.broadcast_to(row - last, step.shape) >= step - s_dev
    return jnp.where((step == 0) | passed, 1.0, 0.0).astype(jnp.bfloat16)


def pack_kernel(geom_ref, ids_ref, out_ref):
    ids = ids_ref[...].astype(jnp.float32)
    out_ref[0:3] = geom_ref[...]
    out_ref[3:4] = jnp.concatenate([ids[i : i + 1] for i in range(ids.shape[0])], 1)


def sym_kernel(s_dev, sym_ref, geom_ref, total_ref, part_ref):
    rows = 2 * sym_ref.shape[1]
    geom = geom_ref[...]
    sums = block_sums(sym_ref[...].reshape(rows, -1), geom, station_marks(geom[3:4], s_dev))
    for moment in range(3):
        total_ref[moment : moment + 1] = sums[moment][0:1]
        for k in range(s_dev):
            part_ref[k, moment : moment + 1] = sums[moment][1 + k : 2 + k]


def anti_total_kernel(geom_ref, anti_ref, sym_ref, sent_ref):
    rows = 2 * anti_ref.shape[1]
    sums = block_sums(anti_ref[...].reshape(rows, -1), geom_ref[...], jnp.ones((8, geom_ref.shape[1]), jnp.bfloat16))
    sent_ref[0] = sym_ref[...]
    for moment in range(3):
        sent_ref[1, moment : moment + 1] = sums[moment][0:1]


def anti_part_kernel(s_dev, geom_ref, anti_ref, after_ref, part_ref):
    geom = geom_ref[...]
    rows = 2 * anti_ref.shape[1]
    sums = block_sums(anti_ref[...].reshape(rows, -1), geom, station_marks(geom[3:4], s_dev))
    for moment in range(3):
        for k in range(s_dev):
            part_ref[k, moment : moment + 1] = sums[moment][1 + k : 2 + k]


def spectrum_kernel(index_ref, rows_ref, arm_ref, after_ref, spec_ref, arms_ref):
    for row in range(2):
        for s in range(arms_ref.shape[1]):
            arms_ref[row, s : s + 1] = jnp.broadcast_to(arm_ref[row : row + 1, s : s + 1], (1, arms_ref.shape[2]))
    gusts, length = spec_ref.shape[0], rows_ref.shape[1]
    index = jnp.broadcast_to(index_ref[...], (gusts, gusts))
    diagonal = lax.broadcasted_iota(jnp.int32, (gusts, gusts), 0) == lax.broadcasted_iota(
        jnp.int32, (gusts, gusts), 1
    )
    samples = jnp.sum(jnp.where(diagonal, index, 0), 1, keepdims=True) + FIRST_GUST
    steps = lax.broadcasted_iota(jnp.int32, (gusts, length), 1)
    phase = steps.astype(jnp.float32) / samples.astype(jnp.float32)
    profile = jnp.where(steps < samples, 0.5 - 0.5 * jnp.cos(2.0 * math.pi * phase), 0.0)
    spec_ref[...] = lax.dot_general(
        profile, rows_ref[...], (((1,), (1,)), ((), ())),
        precision=lax.Precision.HIGHEST, preferred_element_type=jnp.float32,
    )


def history_kernel(sym_ref, anti_ref, arm_ref, spec_ref, basis_ref, out_ref, rows_ref, sems):
    gusts, wide = spec_ref.shape
    freqs = wide // 2
    s_dev = sym_ref.shape[0]
    spec = spec_ref[...]
    lane = lax.broadcasted_iota(jnp.int32, (1, wide), 1)
    crossed = jnp.where(lane < freqs, -1.0, 1.0) * pltpu.roll(spec, freqs, 1)

    def arms(ref, s):
        shear = ref[s, 0:1]
        return [
            shear,
            ref[s, 1:2] - arm_ref[0, s : s + 1] * shear,
            ref[s, 2:3] - arm_ref[1, s : s + 1] * shear,
        ]

    copies = []
    for s in range(s_dev):
        left, right = arms(sym_ref, s), arms(anti_ref, s)
        for comp in range(3):
            blocks = []
            for load in (left[comp] + right[comp], left[comp] - right[comp]):
                turned = pltpu.roll(load, freqs, 1)
                load_re = jnp.where(lane < freqs, load, turned)
                load_im = jnp.where(lane < freqs, turned, load)
                blocks.append((spec * load_re + crossed * load_im).astype(jnp.bfloat16))
            first = (s * 3 + comp) * 2 * gusts
            here = pl.ds(first, 2 * gusts)
            rows_ref[here] = jnp.dot(
                jnp.concatenate(blocks), basis_ref[...], preferred_element_type=jnp.float32
            ).astype(jnp.bfloat16)
            copy = pltpu.make_async_copy(rows_ref.at[here], out_ref.at[here], sems.at[s * 3 + comp])
            copy.start()
            copies.append(copy)
    for copy in copies:
        copy.wait()


def on_device(sym_press, anti_press, box_geom, box_station, station_geom, gust_index):
    devices = lax.axis_size("box")
    me = lax.axis_index("box")
    half = devices // 2
    freqs = sym_press.shape[1]
    box_dev = sym_press.shape[2]
    s_dev = station_geom.shape[1]
    gusts = gust_index.shape[0]
    wide = 2 * freqs
    f32 = jnp.float32

    ids = box_station.reshape(-1, LANES)
    geom = pl.pallas_call(pack_kernel, out_shape=pltpu.VMEM((4, box_dev), f32), name="pack")(box_geom, ids)
    far_geom = swap(geom, "box", half ^ 1)
    near_anti = swap(anti_press, "box", 1)
    sym_total, sym_part = pl.pallas_call(
        lambda *refs: sym_kernel(s_dev, *refs),
        out_shape=(pltpu.VMEM((3, wide), f32), pltpu.VMEM((s_dev, 3, wide), f32)),
        name="sym_sums",
    )(sym_press, in_vmem(geom))
    total = pl.pallas_call(
        anti_total_kernel, out_shape=pltpu.VMEM((2, 3, wide), f32), name="anti_totals"
    )(in_vmem(far_geom), in_vmem(near_anti), in_vmem(sym_total))

    rows = fourier_rows(freqs, NFFT)
    scale = np.where(np.arange(wide) % freqs == 0, 1.0, 2.0)[:, None] / NFFT
    basis = jnp.asarray((rows * scale).astype(np.float32).astype(jnp.bfloat16))

    def later(mask):
        return ((me ^ mask) > me).astype(f32)

    got = swap(total, "box", 1)
    sym_part = sym_part + later(1) * got[0]
    anti_past = (1.0 - later(1)) * got[1]
    total = total + got
    anti_part = pl.pallas_call(
        lambda *refs: anti_part_kernel(s_dev, *refs),
        out_shape=pltpu.VMEM((s_dev, 3, wide), f32),
        name="anti_parts",
    )(in_vmem(far_geom), in_vmem(near_anti), in_vmem(total))
    spec, arm = pl.pallas_call(
        spectrum_kernel, out_shape=(pltpu.VMEM((gusts, wide), f32), pltpu.VMEM((2, s_dev, wide), f32)), name="spectrum"
    )(gust_index.reshape(1, gusts), in_vmem(jnp.asarray(rows)), station_geom, in_vmem(total))
    low, high = 1, half.bit_length() - 1
    while low < high:
        size = min(2, high - low)
        masks = [v << low for v in range(1, 1 << size)]
        parts = [swap(total, "box", mask ^ 1) for mask in masks]
        for mask, part in zip(masks, parts):
            sym_part = sym_part + later(mask) * part[0]
            anti_past = anti_past + later(mask) * part[1]
        total = total + sum(parts)
        low += size
    is_low = (me < half).astype(f32)
    anti_part, spec, arm = lax.optimization_barrier((anti_part, spec, arm))
    got = swap(jnp.concatenate([anti_part + anti_past, total[:1]]), "box", half ^ 1)
    anti_part = got[:-1] + is_low * total[1]
    sym_part = sym_part + is_low * got[-1]

    out = pl.pallas_call(
        history_kernel,
        out_shape=jax.ShapeDtypeStruct((s_dev * 6 * gusts, NFFT), jnp.bfloat16),
        out_specs=pl.BlockSpec(memory_space=pl.ANY),
        scratch_shapes=[
            pltpu.VMEM((s_dev * 6 * gusts, NFFT), jnp.bfloat16),
            pltpu.SemaphoreType.DMA((s_dev * 3,)),
        ],
        name="histories",
    )(in_vmem(sym_part), in_vmem(anti_part), in_vmem(arm), in_vmem(spec), in_vmem(basis))
    return out.reshape(s_dev, 3, 2, gusts, NFFT)


def solution(mesh):
    placed = (
        P("case", None, "box"),
        P("case", None, "box"),
        P(None, "box"),
        P("box"),
        P(None, "box"),
        P(),
    )
    return jax.shard_map(
        on_device,
        mesh=mesh,
        in_specs=placed,
        out_specs=P(("case", "box"), None, None, None, None),
        check_vma=False,
    )
```

```python
import math

import jax
import jax.numpy as jnp
import numpy as np
from jax import lax
from jax.experimental import pallas as pl
from jax.experimental.pallas import tpu as pltpu
from jax.sharding import PartitionSpec as P

NFFT = 512
FIRST_GUST = 8
LANES = 128


def swap(block, axis, mask):
    count = lax.axis_size(axis)
    return lax.ppermute(block, axis, [(i, i ^ mask) for i in range(count)])


def in_vmem(array):
    return pltpu.with_memory_space_constraint(array, pltpu.VMEM)


def fourier_rows(freqs, length):
    turns = np.arange(freqs)[:, None] * np.arange(length)[None, :] % length
    angle = turns * (2.0 * math.pi / length)
    return np.concatenate([np.cos(angle), -np.sin(angle)]).astype(np.float32)


def block_sums(press, geom, marks):
    area = geom[0:1]
    out = []
    for moment in range(3):
        weight = area if moment == 0 else area * geom[moment : moment + 1]
        terms = (press * weight).astype(jnp.bfloat16)
        out.append(
            lax.dot_general(marks, terms, (((1,), (1,)), ((), ())), preferred_element_type=jnp.float32)
        )
    return out


def station_marks(ids, s_dev):
    row = ids
    step = lax.broadcasted_iota(jnp.int32, (8, row.shape[1]), 0).astype(jnp.float32)
    last = row[:, row.shape[1] - 1 :]
    passed = jnp.broadcast_to(row - last, step.shape) >= step - s_dev
    return jnp.where((step == 0) | passed, 1.0, 0.0).astype(jnp.bfloat16)


def pack_kernel(geom_ref, ids_ref, out_ref):
    ids = ids_ref[...].astype(jnp.float32)
    out_ref[0:3] = geom_ref[...]
    out_ref[3:4] = jnp.concatenate([ids[i : i + 1] for i in range(ids.shape[0])], 1)


def sym_kernel(s_dev, sym_ref, geom_ref, total_ref, part_ref):
    rows = 2 * sym_ref.shape[1]
    geom = geom_ref[...]
    sums = block_sums(sym_ref[...].reshape(rows, -1), geom, station_marks(geom[3:4], s_dev))
    for moment in range(3):
        total_ref[moment : moment + 1] = sums[moment][0:1]
        for k in range(s_dev):
            part_ref[k, moment : moment + 1] = sums[moment][1 + k : 2 + k]


def anti_total_kernel(geom_ref, anti_ref, sym_ref, sent_ref):
    rows = 2 * anti_ref.shape[1]
    sums = block_sums(anti_ref[...].reshape(rows, -1), geom_ref[...], jnp.ones((8, geom_ref.shape[1]), jnp.bfloat16))
    sent_ref[0] = sym_ref[...]
    for moment in range(3):
        sent_ref[1, moment : moment + 1] = sums[moment][0:1]


def anti_part_kernel(s_dev, geom_ref, anti_ref, after_ref, part_ref):
    geom = geom_ref[...]
    rows = 2 * anti_ref.shape[1]
    sums = block_sums(anti_ref[...].reshape(rows, -1), geom, station_marks(geom[3:4], s_dev))
    for moment in range(3):
        for k in range(s_dev):
            part_ref[k, moment : moment + 1] = sums[moment][1 + k : 2 + k]


def spectrum_kernel(index_ref, rows_ref, arm_ref, after_ref, basis_ref, spec_ref, arms_ref):
    for row in range(2):
        for s in range(arms_ref.shape[1]):
            arms_ref[row, s : s + 1] = jnp.broadcast_to(arm_ref[row : row + 1, s : s + 1], (1, arms_ref.shape[2]))
    gusts, length = spec_ref.shape[0], rows_ref.shape[1]
    index = jnp.broadcast_to(index_ref[...], (gusts, gusts))
    diagonal = lax.broadcasted_iota(jnp.int32, (gusts, gusts), 0) == lax.broadcasted_iota(
        jnp.int32, (gusts, gusts), 1
    )
    samples = jnp.sum(jnp.where(diagonal, index, 0), 1, keepdims=True) + FIRST_GUST
    steps = lax.broadcasted_iota(jnp.int32, (gusts, length), 1)
    phase = steps.astype(jnp.float32) / samples.astype(jnp.float32)
    profile = jnp.where(steps < samples, 0.5 - 0.5 * jnp.cos(2.0 * math.pi * phase), 0.0)
    spec_ref[...] = lax.dot_general(
        profile, rows_ref[...], (((1,), (1,)), ((), ())),
        precision=lax.Precision.HIGHEST, preferred_element_type=jnp.float32,
    )


def history_kernel(sym_ref, anti_ref, arm_ref, spec_ref, basis_ref, out_ref, rows_ref, sems):
    gusts, wide = spec_ref.shape
    freqs = wide // 2
    s_dev = sym_ref.shape[0]
    spec = spec_ref[...]
    lane = lax.broadcasted_iota(jnp.int32, (1, wide), 1)
    crossed = jnp.where(lane < freqs, -1.0, 1.0) * pltpu.roll(spec, freqs, 1)

    def arms(ref, s):
        shear = ref[s, 0:1]
        return [
            shear,
            ref[s, 1:2] - arm_ref[0, s : s + 1] * shear,
            ref[s, 2:3] - arm_ref[1, s : s + 1] * shear,
        ]

    copies = []
    for s in range(s_dev):
        left, right = arms(sym_ref, s), arms(anti_ref, s)
        for comp in range(3):
            blocks = []
            for load in (left[comp] + right[comp], left[comp] - right[comp]):
                turned = pltpu.roll(load, freqs, 1)
                load_re = jnp.where(lane < freqs, load, turned)
                load_im = jnp.where(lane < freqs, turned, load)
                blocks.append((spec * load_re + crossed * load_im).astype(jnp.bfloat16))
            first = (s * 3 + comp) * 2 * gusts
            here = pl.ds(first, 2 * gusts)
            rows_ref[here] = jnp.dot(
                jnp.concatenate(blocks), basis_ref[...], preferred_element_type=jnp.float32
            ).astype(jnp.bfloat16)
            copy = pltpu.make_async_copy(rows_ref.at[here], out_ref.at[here], sems.at[s * 3 + comp])
            copy.start()
            copies.append(copy)
    for copy in copies:
        copy.wait()


def on_device(sym_press, anti_press, box_geom, box_station, station_geom, gust_index):
    devices = lax.axis_size("box")
    me = lax.axis_index("box")
    half = devices // 2
    freqs = sym_press.shape[1]
    box_dev = sym_press.shape[2]
    s_dev = station_geom.shape[1]
    gusts = gust_index.shape[0]
    wide = 2 * freqs
    f32 = jnp.float32

    ids = box_station.reshape(-1, LANES)
    geom = pl.pallas_call(pack_kernel, out_shape=pltpu.VMEM((4, box_dev), f32), name="pack")(box_geom, ids)
    far_geom = swap(geom, "box", half ^ 1)
    near_anti = swap(anti_press, "box", 1)
    sym_total, sym_part = pl.pallas_call(
        lambda *refs: sym_kernel(s_dev, *refs),
        out_shape=(pltpu.VMEM((3, wide), f32), pltpu.VMEM((s_dev, 3, wide), f32)),
        name="sym_sums",
    )(sym_press, in_vmem(geom))
    total = pl.pallas_call(
        anti_total_kernel, out_shape=pltpu.VMEM((2, 3, wide), f32), name="anti_totals"
    )(in_vmem(far_geom), in_vmem(near_anti), in_vmem(sym_total))

    rows = fourier_rows(freqs, NFFT)
    scale = np.where(np.arange(wide) % freqs == 0, 1.0, 2.0)[:, None] / NFFT
    basis = jnp.asarray((rows * scale).astype(np.float32).astype(jnp.bfloat16))

    def later(mask):
        return ((me ^ mask) > me).astype(f32)

    got = swap(total, "box", 1)
    sym_part = sym_part + later(1) * got[0]
    anti_past = (1.0 - later(1)) * got[1]
    total = total + got
    anti_part = pl.pallas_call(
        lambda *refs: anti_part_kernel(s_dev, *refs),
        out_shape=pltpu.VMEM((s_dev, 3, wide), f32),
        name="anti_parts",
    )(in_vmem(far_geom), in_vmem(near_anti), in_vmem(total))
    spec, arm = pl.pallas_call(
        spectrum_kernel, out_shape=(pltpu.VMEM((gusts, wide), f32), pltpu.VMEM((2, s_dev, wide), f32)), name="spectrum"
    )(gust_index.reshape(1, gusts), in_vmem(jnp.asarray(rows)), station_geom, in_vmem(total), in_vmem(basis))
    low, high = 1, half.bit_length() - 1
    while low < high:
        size = min(2, high - low)
        masks = [v << low for v in range(1, 1 << size)]
        parts = [swap(total, "box", mask ^ 1) for mask in masks]
        for mask, part in zip(masks, parts):
            sym_part = sym_part + later(mask) * part[0]
            anti_past = anti_past + later(mask) * part[1]
        total = total + sum(parts)
        low += size
    is_low = (me < half).astype(f32)
    anti_part, spec, arm = lax.optimization_barrier((anti_part, spec, arm))
    got = swap(jnp.concatenate([anti_part + anti_past, total[:1]]), "box", half ^ 1)
    anti_part = got[:-1] + is_low * total[1]
    sym_part = sym_part + is_low * got[-1]

    out = pl.pallas_call(
        history_kernel,
        out_shape=jax.ShapeDtypeStruct((s_dev * 6 * gusts, NFFT), jnp.bfloat16),
        out_specs=pl.BlockSpec(memory_space=pl.ANY),
        scratch_shapes=[
            pltpu.VMEM((s_dev * 6 * gusts, NFFT), jnp.bfloat16),
            pltpu.SemaphoreType.DMA((s_dev * 3,)),
        ],
        name="histories",
    )(in_vmem(sym_part), in_vmem(anti_part), in_vmem(arm), in_vmem(spec), in_vmem(basis))
    return out.reshape(s_dev, 3, 2, gusts, NFFT)


def solution(mesh):
    placed = (
        P("case", None, "box"),
        P("case", None, "box"),
        P(None, "box"),
        P("box"),
        P(None, "box"),
        P(),
    )
    return jax.shard_map(
        on_device,
        mesh=mesh,
        in_specs=placed,
        out_specs=P(("case", "box"), None, None, None, None),
        check_vma=False,
    )
```
